1024 devices in a mesh: dp: 64 (over x, z), tensor: 8 (over y), side: 2 (over core).
Axes of the slice: x: 8, y: 8, z: 8, core: 2. Of those that a mesh axis runs over, the one named last changes fastest.
Arguments:
- tokens: bfloat16 [8192, 4096], P('dp', ('tensor', 'side')), may hold values from -6 to 6
- gain: bfloat16 [4096], P(('tensor', 'side')), may hold values from 0.25 to 1.75
- router: bfloat16 [4096, 128], P(('tensor', 'side'))
- routes: int32 [8192, 8], P('dp'), may hold values from 0 to 127, as said below
- w_gate: bfloat16 [128, 4096, 768], P(('dp', 'side'), None, 'tensor'), may hold values from -0.09375 to 0.09375
- w_up: bfloat16 [128, 4096, 768], P(('dp', 'side'), None, 'tensor'), may hold values from -0.09375 to 0.09375
- w_down: bfloat16 [128, 768, 4096], P(('dp', 'side'), 'tensor'), may hold values from -0.21875 to 0.21875
Outputs:
- mixed: bfloat16 [8192, 4096], P('dp', ('tensor', 'side'))
The draws below stay inside these ranges and needn't reach their ends.
Inputs may be any that keep to these rules, and one draw needn't show every extreme that they name: `routes`: each row names 8 different experts. In each aligned block of 128 rows (the tokens of one dp index) no expert is named by more than 10 rows, and some expert is named by exactly 10.
All inputs are finite; a program needn't handle non-finite values.
Results may differ from the reference program's by a relative error of at most 0.02.
Values may be sent and summed in bfloat16 or wider, within the bound.
A program may use at most 64 MiB of HBM per device.

```python
import jax
import jax.numpy as jnp
from jax import lax

D = 4096
FF = 768
TOP = 8
TOK_DEV = 128
EXPERTS = 128
CAP = 10
TOKENS = 8192


def draw_router(key, part):
    key = jax.random.fold_in(key, 5)
    first = jax.random.fold_in(key, 0)
    base = jax.random.normal(first, (D, EXPERTS), jnp.float32) * D ** (-0.5)
    return base.astype(jnp.bfloat16)


def draw_routes(key, part):
    key = jax.random.fold_in(key, 7)
    k_rank, k_score, k_full, k_rows, k_cols = jax.random.split(key, 5)
    blocks = TOKENS // TOK_DEV
    pairs = TOK_DEV * TOP
    rank = jax.random.permutation(k_rank, EXPERTS).astype(jnp.int32)
    expert_ids = jnp.arange(EXPERTS, dtype=jnp.int32)
    raw = jax.random.randint(k_score, (blocks, EXPERTS), 0, 1 << 16, jnp.int32)
    scores = raw // (1 + rank[None, :] * 4 // EXPERTS) * EXPERTS + expert_ids[None, :]
    order = jnp.argsort(-scores, axis=1).astype(jnp.int32)
    most_full = 3 * pairs // (4 * CAP)
    full = most_full - jax.random.randint(k_full, (blocks, 1), 0, most_full // 4 + 1, jnp.int32)
    rest = EXPERTS - full
    spare = pairs - full * CAP
    base_count = spare // rest
    extra = spare % rest
    position = expert_ids[None, :]
    tail = position - full
    counts = jnp.where(position < full, CAP, base_count + (tail < extra).astype(jnp.int32)).astype(jnp.int32)
    ends = jnp.cumsum(counts, axis=1).astype(jnp.int32)
    places = jnp.arange(pairs, dtype=jnp.int32)
    index = jnp.sum((ends[:, None, :] <= places[None, :, None]).astype(jnp.int32), axis=2).astype(jnp.int32)
    named = jnp.take_along_axis(order, index, axis=1)
    grid = named.reshape(blocks, TOP, TOK_DEV).transpose(0, 2, 1)
    row_keys = jax.random.split(k_rows, blocks)
    perms = jax.vmap(lambda one: jax.random.permutation(one, TOK_DEV))(row_keys).astype(jnp.int32)
    grid = jnp.take_along_axis(grid, perms[:, :, None], axis=1)
    noise = jax.random.randint(k_cols, (blocks, TOK_DEV, TOP), 0, 1 << 16, jnp.int32) * TOP + jnp.arange(TOP, dtype=jnp.int32)
    columns = jnp.argsort(noise, axis=2).astype(jnp.int32)
    grid = jnp.take_along_axis(grid, columns, axis=2)
    return grid.reshape(TOKENS, TOP).astype(jnp.int32)


def levels(rng, dims, shards, smallest, high):
    level = 1.0
    for dim, parts in shards:
        heights = jax.random.uniform(jax.random.fold_in(jax.random.fold_in(rng, 6), dim), (parts,), jnp.float32, smallest / len(shards), high / len(shards))
        level = level * jnp.repeat(jnp.exp(heights), dims[dim] // parts).reshape((-1,) + (1,) * (len(dims) - 1 - dim))
    return level


def gaussian(stream_key, extent, scale, most, cuts=(), kind=jnp.bfloat16):
    result = scale * jax.random.normal(stream_key, extent, jnp.float32)
    if cuts:
        result = result * levels(stream_key, extent, cuts, -0.22, 0.18)
    return jnp.clip(result, -most, most).astype(kind)


def setup_inputs(seed: int = 0) -> dict:
    streams_of = jax.random.split(jax.random.key(seed), 8)
    tokens = gaussian(streams_of[0], (TOKENS, D), 1.0, 6.0, ((0, 64), (1, 16)))
    gain = jnp.clip(1.0 + 0.15 * jax.random.normal(streams_of[1], (D,), jnp.float32), 0.25, 1.75).astype(jnp.bfloat16)
    router = draw_router(jax.random.fold_in(streams_of[7], 71), 0)
    routes = draw_routes(jax.random.fold_in(streams_of[7], 71), 0)
    w_gate = gaussian(streams_of[4], (EXPERTS, D, FF), D ** -0.5, 0.09375, ((0, 128), (2, 8)))
    w_up = gaussian(streams_of[5], (EXPERTS, D, FF), D ** -0.5, 0.09375, ((0, 128), (2, 8)))
    w_down = gaussian(streams_of[6], (EXPERTS, FF, D), FF ** -0.5, 0.21875, ((0, 128), (1, 8)))
    return {"tokens": tokens, "gain": gain, "router": router, "routes": routes, "w_gate": w_gate, "w_up": w_up, "w_down": w_down}


def reference(tokens, gain, router, routes, w_gate, w_up, w_down):
    xf = tokens.astype(jnp.float32)
    gf = gain.astype(jnp.float32)
    rinv = lax.rsqrt(lax.optimization_barrier(jnp.mean(xf * xf, axis=1)) + 1e-06)
    logits = jnp.dot(xf * gf, router.astype(jnp.float32), precision=lax.Precision.HIGHEST) * rinv[:, None]
    normed = (xf * rinv[:, None] * gf).astype(jnp.bfloat16)
    expert_ids = jnp.arange(EXPERTS, dtype=jnp.int32)
    onehot = routes[:, :, None] == expert_ids[None, None, :]
    picked = lax.optimization_barrier(jnp.sum(jnp.where(onehot, logits[:, None, :], 0.0), axis=-1))
    weights = jax.nn.softmax(picked, axis=-1)
    counts = lax.optimization_barrier(jnp.sum(onehot.astype(jnp.int32), axis=1))
    blocks = TOKENS // TOK_DEV
    grouped = counts.reshape(blocks, TOK_DEV, EXPERTS)
    before = (jnp.cumsum(grouped, axis=1) - grouped).reshape(TOKENS, EXPERTS)
    slot = lax.optimization_barrier(jnp.sum(jnp.where(onehot, before[:, None, :], 0), axis=-1)).astype(jnp.int32)
    block_id = (jnp.arange(TOKENS, dtype=jnp.int32) // TOK_DEV).astype(jnp.int32)
    rows_per = blocks * CAP
    flat = (routes * rows_per + block_id[:, None] * CAP + slot).astype(jnp.int32)
    owners = jnp.broadcast_to(jnp.arange(TOKENS, dtype=jnp.int32)[:, None], (TOKENS, TOP))
    source = jnp.zeros((EXPERTS * rows_per,), jnp.int32).at[flat.reshape(-1)].set(owners.reshape(-1))
    filled = jnp.zeros((EXPERTS * rows_per,), jnp.int32).at[flat.reshape(-1)].set(1)

    def expert(index):
        start = (index * rows_per).astype(jnp.int32)
        idx = lax.dynamic_slice_in_dim(source, start, rows_per)
        live = lax.dynamic_slice_in_dim(filled, start, rows_per)
        rows = jnp.where(live[:, None] > 0, normed[idx], jnp.zeros((), jnp.bfloat16))
        gate = jnp.dot(rows, w_gate[index], preferred_element_type=jnp.float32)
        upper = jnp.dot(rows, w_up[index], preferred_element_type=jnp.float32)
        hidden = (jax.nn.silu(gate) * upper).astype(jnp.bfloat16)
        return jnp.dot(hidden, w_down[index], preferred_element_type=jnp.float32).astype(jnp.bfloat16)
    outputs = lax.map(expert, expert_ids).reshape(EXPERTS * rows_per, D)
    mixed = jnp.zeros((TOKENS, D), jnp.float32)
    for choice_k in range(TOP):
        mixed = mixed + weights[:, choice_k:choice_k + 1] * outputs[flat[:, choice_k]].astype(jnp.float32)
    return mixed.astype(jnp.bfloat16)
```

```python
import functools

import jax
import jax.numpy as jnp
from jax import lax
from jax.experimental import pallas as pl
from jax.experimental.pallas import tpu as pltpu
from jax.sharding import PartitionSpec as P

MESH = pl.DeviceIdType.MESH
BF = jnp.bfloat16
F32 = jnp.float32
LANE = 128
HIGH = lax.Precision.HIGHEST
NT = (((1,), (1,)), ((), ()))
TN = (((0,), (0,)), ((), ()))


def dot(a, b, dims=(((1,), (0,)), ((), ())), precision=None):
    return lax.dot_general(a, b, dims, precision=precision, preferred_element_type=F32)


def split_slots(slots):
    return ((0, slots),)


def plane_rows(count, chunks):
    return -(-count * chunks // 16) * 16


def kernel(cfg, *refs):
    n_dp, n_t, slots, groups, toks, feats, experts, top, hid_n = cfg
    it = iter(refs)
    take = lambda n: [next(it) for _ in range(n)]
    tokens, gain, router, routes, w_gate, w_up, w_down, out = take(8)
    xtok, rt, gn, chosen, tmp, lp, lr, lg, ss, wt, wdb, ct, mixs, mixr = take(14)
    ng = len(groups)
    send, recv, send2, recv2, ag, hid, acc, oacc = [take(ng) for _ in range(8)]
    pair_s, pair_r, wd_s, wd_r, lp_s, lp_r, lg_s, lg_r, mix_s, mix_r = take(10)
    dis_s, dis_r, ret_s, ret_r, ss_s, ss_r, ag_s, ag_r, hid_s, hid_r = take(10)

    d, t, s = lax.axis_index("dp"), lax.axis_index("tensor"), lax.axis_index("side")
    nz = 8 if n_dp % 8 == 0 else n_dp
    nx = n_dp // nz
    chunks = 2 * feats // LANE
    per_half = feats // LANE
    piece = toks // n_t
    other = 1 - s

    def dp_peer(i):
        return lax.rem(d // nz + i // nz, nx) * nz + lax.rem(d % nz + i % nz, nz)

    def t_peer(i):
        return lax.rem(t + i, n_t)

    def rcopy(src, dst, ssem, rsem, dev):
        return pltpu.make_async_remote_copy(
            src_ref=src, dst_ref=dst, send_sem=ssem, recv_sem=rsem, device_id=dev, device_id_type=MESH
        )

    def wait_bytes(ref, sem):
        pltpu.make_async_copy(ref, ref, sem).wait()

    barrier = pltpu.get_barrier_semaphore()
    pl.semaphore_signal(barrier, inc=1, device_id=(d, t, other), device_id_type=MESH)

    def greet_t(i, carry):
        pl.semaphore_signal(barrier, inc=1, device_id=(d, t_peer(i), s), device_id_type=MESH)
        return carry

    def greet_dp(i, carry):
        pl.semaphore_signal(barrier, inc=1, device_id=(dp_peer(i), t, s), device_id_type=MESH)
        return carry

    lax.fori_loop(1, n_t, greet_t, 0)
    lax.fori_loop(1, n_dp, greet_dp, 0)

    e_ids = lax.broadcasted_iota(jnp.int32, (toks, experts), 1)
    routes_v = routes[...]
    onehot = jnp.zeros((toks, experts), F32)
    for k in range(top):
        onehot = onehot + jnp.where(routes_v[:, k : k + 1] == e_ids, 1.0, 0.0)
    lower = jnp.where(
        lax.broadcasted_iota(jnp.int32, (toks, toks), 1) < lax.broadcasted_iota(jnp.int32, (toks, toks), 0), 1.0, 0.0
    )
    before = dot(lower.astype(BF), onehot.astype(BF))
    taken = (onehot * (before + 1.0)).astype(BF)

    rows = slots * n_dp
    r_of = lax.broadcasted_iota(jnp.int32, (rows, experts), 0)
    expand = jnp.where(
        lax.broadcasted_iota(jnp.int32, (rows, experts), 1) == 2 * (r_of % n_dp) + s, 1.0, 0.0
    ).astype(BF)
    slot_of = lax.broadcasted_iota(jnp.int32, (rows, toks), 0) // n_dp + 1
    chosen[...] = jnp.where(dot(expand, taken, NT) == slot_of.astype(F32), 1.0, 0.0).astype(BF)
    gn[s] = jnp.broadcast_to(gain[...].astype(F32), (8, feats))
    xtok[s] = tokens[...]
    rt[s] = router[...]
    tmp[...] = jnp.zeros_like(tmp)

    pl.semaphore_wait(barrier, 1 + (n_t - 1) + (n_dp - 1))

    pairs = [
        rcopy(ref, ref, pair_s.at[i], pair_r.at[i], (d, t, other))
        for i, ref in enumerate((xtok.at[s], rt.at[s], gn.at[s]))
    ]
    for c in pairs:
        c.start()

    def wd_send(i, carry):
        p = t_peer(i)
        cols = pl.ds(pl.multiple_of(p * 2 * feats, 2 * feats), 2 * feats)
        rcopy(w_down.at[0, :, cols], wdb.at[t], wd_s, wd_r, (d, p, s)).start()
        return carry

    lax.fori_loop(1, n_t, wd_send, 0)
    wdb[t] = w_down[0, :, pl.ds(pl.multiple_of(t * 2 * feats, 2 * feats), 2 * feats)]

    def pack(value_of, g, dst):
        s0, ns = groups[g]
        pr = plane_rows(ns, chunks)
        for c in range(chunks):
            v = value_of(c)
            for q in range(ns):
                tmp[pl.ds(c * ns + q, n_dp, stride=pr), :] = v[q * n_dp : (q + 1) * n_dp]
        dst[...] = tmp[: n_dp * pr].astype(BF)

    def exchange(g, src, dst, ssem, rsem):
        pr = plane_rows(groups[g][1], chunks)

        def plane(i):
            return pl.ds(pl.multiple_of(i * pr, pr), pr)

        def one(i, carry):
            p = dp_peer(i)
            rcopy(src.at[plane(p)], dst.at[plane(d)], ssem, rsem, (p, t, s)).start()
            return carry

        lax.fori_loop(1, n_dp, one, 0)
        dst[plane(d), :] = src[plane(d), :]

    def exchange_wait(g, dst, sem):
        pr = plane_rows(groups[g][1], chunks)
        wait_bytes(dst.at[pl.ds(0, (n_dp - 1) * pr)], sem)

    pairs[0].wait_recv()
    for g, (s0, ns) in enumerate(groups):
        sel = chosen[s0 * n_dp : (s0 + ns) * n_dp]
        halves = [dot(sel, xtok[h]) for h in range(2)]
        pack(lambda c: halves[c // per_half][:, (c % per_half) * LANE : (c % per_half + 1) * LANE], g, send[g])
        exchange(g, send[g], recv[g], dis_s.at[g], dis_r.at[g])

    for c in pairs[1:]:
        c.wait_recv()
    part = jnp.zeros((toks, experts), F32)
    sq = jnp.zeros((toks, 1), F32)
    for h in range(2):
        xf = xtok[h].astype(F32)
        sq = sq + jnp.sum(xf * xf, axis=1, keepdims=True)
        part = part + dot(xf * gn[h][0:1], rt[h].astype(F32), precision=HIGH)
    for j in range(n_t):
        lp[j, 0] = part[j * piece : (j + 1) * piece]
        lp[j, 1] = jnp.broadcast_to(sq[j * piece : (j + 1) * piece], (piece, experts))

    def lp_send(i, carry):
        p = t_peer(i)
        rcopy(lp.at[p], lr.at[t], lp_s, lp_r, (d, p, s)).start()
        return carry

    lax.fori_loop(1, n_t, lp_send, 0)
    lr[t] = lp[t]

    eye = jnp.where(
        lax.broadcasted_iota(jnp.int32, (hid_n, hid_n), 0) == lax.broadcasted_iota(jnp.int32, (hid_n, hid_n), 1), 1.0, 0.0
    ).astype(BF)

    def turn(j, carry):
        for h in range(2):
            k0 = pl.ds(pl.multiple_of(j * 2 * feats + h * feats, feats), feats)
            wt[j, h, 0:hid_n] = dot(eye, w_gate[0, k0, :], NT).astype(BF)
            wt[j, h, hid_n : 2 * hid_n] = dot(eye, w_up[0, k0, :], NT).astype(BF)
        return carry

    lax.fori_loop(0, n_t, turn, 0)

    wait_bytes(lr.at[pl.ds(0, n_t - 1)], lp_r)
    tot = lr[0]
    for j in range(1, n_t):
        tot = tot + lr[j]
    width = 2 * feats * n_t
    lg[t] = tot[0] * lax.rsqrt(tot[1] / width + 1e-06)

    def lg_send(i, carry):
        rcopy(lg.at[t], lg.at[t], lg_s, lg_r, (d, t_peer(i), s)).start()
        return carry

    lax.fori_loop(1, n_t, lg_send, 0)

    right, left = t_peer(1), t_peer(n_t - 1)
    hops = n_t // 2

    def ring(ref_of, ssem, rsem, halves, hop, direction, h):
        origin = t_peer(n_t - (hop - 1)) if direction == 0 else t_peer(hop - 1)
        ref = ref_of(origin, h)
        k = (direction * hops + hop - 1) * halves + h
        return rcopy(ref, ref, ssem.at[k], rsem.at[k], (d, right if direction == 0 else left, s))

    def arrived(ref_of, ssem, rsem, halves, hop, direction, h):
        origin = t_peer(n_t - hop) if direction == 0 else t_peer(hop)
        ref = ref_of(origin, h)
        k = (direction * hops + hop - 1) * halves + h
        rcopy(ref, ref, ssem.at[k], rsem.at[k], (d, right if direction == 0 else left, s)).wait_recv()
        return origin

    def legs(hop):
        if hop < hops:
            return [(h, direction) for h in range(2) for direction in range(2)]
        return [(0, 0), (1, 1)]

    def unpack(src, g, use):
        s0, ns = groups[g]
        pr = plane_rows(ns, chunks)
        tmp[: n_dp * pr] = src[...].astype(F32)
        for q in range(ns):
            use(q, [tmp[pl.ds(c * ns + q, n_dp, stride=pr), :] for c in range(chunks)])

    for g, (s0, ns) in enumerate(groups):
        n_rows = ns * n_dp
        exchange_wait(g, recv[g], dis_r.at[g])
        squares = []

        def scale(q, cols):
            squares.append(sum(v * v for v in cols))
            for c, v in enumerate(cols):
                h, l0 = c // per_half, (c % per_half) * LANE
                ag[g][t, h, q * n_dp : (q + 1) * n_dp, l0 : l0 + LANE] = (v * gn[h][0:1, l0 : l0 + LANE]).astype(BF)

        unpack(recv[g], g, scale)
        ref_of = lambda o, h, g=g: ag[g].at[o, h]
        for h, direction in legs(1) if hops > 1 else [(0, 0), (1, 1)]:
            ring(ref_of, ag_s.at[g], ag_r.at[g], 2, 1, direction, h).start()
        ones = jnp.ones((8, LANE), F32)
        cols = pl.ds(s0 * n_dp, n_rows)
        for q in range(ns):
            ss[t, :, (s0 + q) * n_dp : (s0 + q + 1) * n_dp] = dot(ones, squares[q], NT, precision=HIGH)

        def ss_send(i, carry):
            rcopy(ss.at[t, :, cols], ss.at[t, :, cols], ss_s.at[g], ss_r.at[g], (d, t_peer(i), s)).start()
            return carry

        lax.fori_loop(1, n_t, ss_send, 0)
        acc[g][...] = dot(wt[t, 0], ag[g][t, 0], NT) + dot(wt[t, 1], ag[g][t, 1], NT)

    wait_bytes(lg.at[pl.ds(0, n_t - 1)], lg_r)
    logits = jnp.concatenate([lg[j] for j in range(n_t)], axis=0)
    masked = jnp.where(onehot > 0.0, logits, -jnp.inf)
    ex = jnp.exp(masked - jnp.max(masked, axis=1, keepdims=True))
    weights = ex / jnp.sum(ex, axis=1, keepdims=True)
    r_of = lax.broadcasted_iota(jnp.int32, (experts, rows), 1)
    expand_t = jnp.where(
        lax.broadcasted_iota(jnp.int32, (experts, rows), 0) == 2 * (r_of % n_dp) + s, 1.0, 0.0
    ).astype(BF)
    slot_of = lax.broadcasted_iota(jnp.int32, (toks, rows), 1) // n_dp + 1
    mine = dot(taken, expand_t) == slot_of.astype(F32)
    w_hi = weights.astype(BF)
    w_lo = (weights - w_hi.astype(F32)).astype(BF)
    ct[0] = jnp.where(mine, dot(w_hi, expand_t), 0.0).astype(BF)
    ct[1] = jnp.where(mine, dot(w_lo, expand_t), 0.0).astype(BF)
    wait_bytes(wdb.at[pl.ds(0, n_t - 1)], wd_r)

    for g, (s0, ns) in enumerate(groups):
        n_rows = ns * n_dp
        ref_of = lambda o, h, g=g: ag[g].at[o, h]
        for hop in range(1, hops + 1):
            coming = legs(hop)
            going = legs(hop + 1) if hop < hops else []
            for h, direction in coming:
                origin = arrived(ref_of, ag_s.at[g], ag_r.at[g], 2, hop, direction, h)
                if (h, direction) in going:
                    ring(ref_of, ag_s.at[g], ag_r.at[g], 2, hop + 1, direction, h).start()
                acc[g][...] += dot(wt[origin, h], ag[g][origin, h], NT)
        if g == 0:
            pass
        cols = slice(s0 * n_dp, (s0 + ns) * n_dp)
        wait_bytes(ss.at[pl.ds(0, n_t - 1), :, pl.ds(s0 * n_dp, n_rows)], ss_r.at[g])
        total = ss[0, 0:1, cols]
        for j in range(1, n_t):
            total = total + ss[j, 0:1, cols]
        rinv = lax.rsqrt(total / width + 1e-06)
        gate = acc[g][0:hid_n] * rinv
        hid[g][t] = (gate * jax.nn.sigmoid(gate) * (acc[g][hid_n : 2 * hid_n] * rinv)).astype(BF)

        half = hid_n // 2

        def hid_ref(o, h, g=g):
            return hid[g].at[o] if h is None else hid[g].at[o, pl.ds(h * half, half)]

        def hid_legs(hop):
            return [(None, 0), (None, 1)] if hop < hops else [(0, 0), (1, 1)]

        def hid_copy(hop, direction, h, incoming):
            step = hop if incoming else hop - 1
            origin = t_peer((n_t - step) % n_t) if direction == 0 else t_peer(step)
            ref = hid_ref(origin, h)
            k = direction * hops + hop - 1
            return origin, rcopy(
                ref, ref, hid_s.at[g, k], hid_r.at[g, k], (d, right if direction == 0 else left, s)
            )

        for h, direction in hid_legs(1):
            hid_copy(1, direction, h, False)[1].start()
        oacc[g][...] = dot(hid[g][t], wdb[t], TN)
        for hop in range(1, hops + 1):
            got = []
            for h, direction in hid_legs(hop):
                origin, c = hid_copy(hop, direction, h, True)
                c.wait_recv()
                got.append(origin)
                if hop < hops:
                    nh = None if hop + 1 < hops else direction
                    hid_copy(hop + 1, direction, nh, False)[1].start()
            for origin in got if hop < hops else got[:1]:
                oacc[g][...] += dot(hid[g][origin], wdb[origin], TN)
        pack(lambda c: oacc[g][:, c * LANE : (c + 1) * LANE], g, send2[g])
        exchange(g, send2[g], recv2[g], ret_s.at[g], ret_r.at[g])

    for g, (s0, ns) in enumerate(groups):
        n_rows = ns * n_dp
        exchange_wait(g, recv2[g], ret_r.at[g])

        def keep(q, cols):
            for c, v in enumerate(cols):
                oacc[g][q * n_dp : (q + 1) * n_dp, c * LANE : (c + 1) * LANE] = v

        unpack(recv2[g], g, keep)
        for h in range(2):
            z = oacc[g][:, h * feats : (h + 1) * feats].astype(BF)
            cols = slice(s0 * n_dp, (s0 + ns) * n_dp)
            m = dot(ct[0, :, cols], z) + dot(ct[1, :, cols], z)
            mixs[h] = m if g == 0 else mixs[h] + m
    last = rcopy(mixs.at[other], mixr, mix_s, mix_r, (d, t, other))
    last.start()
    last.wait_recv()
    out[...] = (mixs[s] + mixr[...]).astype(BF)

    last.wait_send()
    for c in pairs:
        c.wait_send()
    wait_bytes(wdb.at[pl.ds(0, n_t - 1)], wd_s)
    wait_bytes(lr.at[pl.ds(0, n_t - 1)], lp_s)
    wait_bytes(lg.at[pl.ds(0, n_t - 1)], lg_s)
    for g, (s0, ns) in enumerate(groups):
        exchange_wait(g, recv[g], dis_s.at[g])
        exchange_wait(g, recv2[g], ret_s.at[g])
        wait_bytes(ss.at[pl.ds(0, n_t - 1), :, pl.ds(s0 * n_dp, ns * n_dp)], ss_s.at[g])
        ref_of = lambda o, h, g=g: ag[g].at[o, h]
        for hop in range(1, hops + 1):
            for h, direction in legs(hop):
                ring(ref_of, ag_s.at[g], ag_r.at[g], 2, hop, direction, h).wait_send()
            for direction in range(2):
                h = None if hop < hops else direction
                ref = hid[g].at[t] if h is None else hid[g].at[t, pl.ds(h * (hid_n // 2), hid_n // 2)]
                pltpu.make_async_copy(ref, ref, hid_s.at[g, direction * hops + hop - 1]).wait()


def body(tokens, gain, router, routes, w_gate, w_up, w_down):
    toks, feats = tokens.shape
    top = routes.shape[1]
    n_dp, n_t, n_side = (lax.axis_size(a) for a in ("dp", "tensor", "side"))
    experts = n_dp * n_side
    slots = min(toks, max(2, toks * top * 5 // (experts * 4)))
    hid_n = w_gate.shape[2]
    groups = split_slots(slots)
    chunks = 2 * feats // LANE
    n_rows = [ns * n_dp for _, ns in groups]
    planes = [n_dp * plane_rows(ns, chunks) for _, ns in groups]
    rows = slots * n_dp
    hops = n_t // 2
    piece = toks // n_t
    cfg = (n_dp, n_t, slots, groups, toks, feats, experts, top, hid_n)
    vm = pltpu.VMEM
    dma = pltpu.SemaphoreType.DMA
    ng = len(groups)
    plane_bufs = [vm((p, LANE), BF) for p in planes]
    scratch = (
        [
            vm((2, toks, feats), BF),
            vm((2, feats, experts), BF),
            vm((2, 8, feats), F32),
            vm((rows, toks), BF),
            vm((max(planes), LANE), F32),
            vm((n_t, 2, piece, experts), F32),
            vm((n_t, 2, piece, experts), F32),
            vm((n_t, piece, experts), F32),
            vm((n_t, 8, rows), F32),
            vm((n_t, 2, 2 * hid_n, feats), BF),
            vm((n_t, hid_n, 2 * feats), BF),
            vm((2, toks, rows), BF),
            vm((2, toks, feats), F32),
            vm((toks, feats), F32),
        ]
        + plane_bufs * 4
        + [vm((n_t, 2, n, feats), BF) for n in n_rows]
        + [vm((n_t, hid_n, n), BF) for n in n_rows]
        + [vm((2 * hid_n, n), F32) for n in n_rows]
        + [vm((n, 2 * feats), F32) for n in n_rows]
        + [dma((3,)), dma((3,))]
        + [dma] * 8
        + [dma((ng,))] * 6
        + [dma((ng, 4 * hops))] * 2
        + [dma((ng, 2 * hops))] * 2
    )
    return pl.pallas_call(
        functools.partial(kernel, cfg),
        out_shape=jax.ShapeDtypeStruct((toks, feats), BF),
        in_specs=[pl.BlockSpec(memory_space=vm)] * 7,
        out_specs=pl.BlockSpec(memory_space=vm),
        scratch_shapes=scratch,
        compiler_params=pltpu.CompilerParams(
            collective_id=0, has_side_effects=True, vmem_limit_bytes=56 * 1024 * 1024
        ),
        name="routed_experts",
    )(tokens, gain.reshape(1, feats), router, routes, w_gate, w_up, w_down)


def solution(mesh):
    placed = (
        P("dp", ("tensor", "side")),
        P(("tensor", "side")),
        P(("tensor", "side"), None),
        P("dp", None),
        P(("dp", "side"), None, "tensor"),
        P(("dp", "side"), None, "tensor"),
        P(("dp", "side"), "tensor", None),
    )
    return jax.shard_map(
        body, mesh=mesh, in_specs=placed, out_specs=P("dp", ("tensor", "side")), check_vma=False
    )
```

```python
import functools

import jax
import jax.numpy as jnp
from jax import lax
from jax.experimental import pallas as pl
from jax.experimental.pallas import tpu as pltpu
from jax.sharding import PartitionSpec as P

MESH = pl.DeviceIdType.MESH
BF = jnp.bfloat16
F32 = jnp.float32
LANE = 128
HIGH = lax.Precision.HIGHEST
NT = (((1,), (1,)), ((), ()))
TN = (((0,), (0,)), ((), ()))


def dot(a, b, dims=(((1,), (0,)), ((), ())), precision=None):
    return lax.dot_general(a, b, dims, precision=precision, preferred_element_type=F32)


def split_slots(slots):
    return ((0, slots),)


def plane_rows(count, chunks):
    return -(-count * chunks // 8) * 8


def schedule(ng, gather_hops, unit_hops):
    steps = [("rows", 0)] + [("gather", 0, k) for k in range(1, gather_hops)] + [("far", 0, 0), ("far", 0, 1)]
    steps += [("gather", 0, gather_hops), ("hidden", 0)]
    return steps + [("units", 0, k) for k in range(1, unit_hops + 1)] + [("back", 0)]


def kernel(cfg, *refs):
    n_dp, n_t, slots, groups, toks, feats, experts, top, hid_n = cfg
    it = iter(refs)
    take = lambda n: [next(it) for _ in range(n)]
    tokens, gain, router, routes, w_gate, w_up, w_down, out = take(8)
    xtok, xg, far, rt, gn, chosen, tmp, lp, lr, lg, ss, wt, wdb, ct, mixs, mixr = take(16)
    ng = len(groups)
    send, recv = take(3 * ng), take(3 * ng)
    send2, recv2, ag, hid, acc, oacc = [take(ng) for _ in range(6)]
    pair_s, pair_r, far_s, far_r, wd_s, wd_r, lp_s, lp_r, lg_s, lg_r, mix_s, mix_r, wt_r, wl_r = take(14)
    dis_s, dis_r, ret_s, ret_r, ss_s, ss_r, ag_s, ag_r, hid_s, hid_r = take(10)

    d, t, s = lax.axis_index("dp"), lax.axis_index("tensor"), lax.axis_index("side")
    nz = 8 if n_dp % 8 == 0 else n_dp
    nx = n_dp // nz
    chunks = 2 * feats // LANE
    per_half = feats // LANE
    piece = toks // n_t
    width = 2 * feats * n_t
    rows = slots * n_dp
    other = 1 - s
    gather_hops, unit_hops = n_t // 2 - 1, n_t // 2
    left_over = []

    def dp_peer(i):
        return lax.rem(d // nz + i // nz, nx) * nz + lax.rem(d % nz + i % nz, nz)

    def t_peer(i):
        return lax.rem(t + i, n_t)

    def rcopy(src, dst, ssem, rsem, dev):
        return pltpu.make_async_remote_copy(
            src_ref=src, dst_ref=dst, send_sem=ssem, recv_sem=rsem, device_id=dev, device_id_type=MESH
        )

    def wait_bytes(ref, sem):
        pltpu.make_async_copy(ref, ref, sem).wait()

    def later(f, *args):
        left_over.append(lambda: f(*args))

    barrier = pltpu.get_barrier_semaphore()
    pl.semaphore_signal(barrier, inc=1, device_id=(d, t, other), device_id_type=MESH)

    def greet_t(i, carry):
        pl.semaphore_signal(barrier, inc=1, device_id=(d, t_peer(i), s), device_id_type=MESH)
        return carry

    def greet_dp(i, carry):
        pl.semaphore_signal(barrier, inc=1, device_id=(dp_peer(i), t, s), device_id_type=MESH)
        return carry

    lax.fori_loop(1, n_t, greet_t, 0)
    lax.fori_loop(1, n_dp, greet_dp, 0)

    def weights_in(j, carry):
        for h in range(2):
            k0 = pl.ds(pl.multiple_of(j * 2 * feats + h * feats, feats), feats)
            pltpu.make_async_copy(w_gate.at[0, :, k0], wt.at[j, h, pl.ds(0, hid_n)], wt_r).start()
            pltpu.make_async_copy(w_up.at[0, :, k0], wt.at[j, h, pl.ds(hid_n, hid_n)], wt_r).start()
        return carry

    lax.fori_loop(0, n_t, weights_in, 0)
    down_cols = lambda p: pl.ds(pl.multiple_of(p * 2 * feats, 2 * feats), 2 * feats)
    own_down = pltpu.make_async_copy(w_down.at[0, :, down_cols(t)], wdb.at[t], wl_r)
    own_down.start()

    e_ids = lax.broadcasted_iota(jnp.int32, (experts, toks), 0)
    routes_v = routes[...]
    onehot = jnp.zeros((experts, toks), F32)
    for k in range(top):
        onehot = onehot + jnp.where(routes_v[k : k + 1, :] == e_ids, 1.0, 0.0)
    earlier = jnp.where(
        lax.broadcasted_iota(jnp.int32, (toks, toks), 0) < lax.broadcasted_iota(jnp.int32, (toks, toks), 1), 1.0, 0.0
    )
    before = dot(onehot.astype(BF), earlier.astype(BF))
    taken = (onehot * (before + 1.0)).astype(BF)

    r_of = lax.broadcasted_iota(jnp.int32, (rows, experts), 0)
    expand = jnp.where(
        lax.broadcasted_iota(jnp.int32, (rows, experts), 1) == 2 * (r_of % n_dp) + s, 1.0, 0.0
    ).astype(BF)
    slot_of = lax.broadcasted_iota(jnp.int32, (rows, toks), 0) // n_dp + 1
    chosen[...] = jnp.where(dot(expand, taken) == slot_of.astype(F32), 1.0, 0.0).astype(BF)
    gn[s] = jnp.broadcast_to(gain[...].astype(F32), (8, feats))
    xtok[s] = tokens[...]
    xg[...] = (tokens[...].astype(F32) * gn[s, 0:1]).astype(BF)
    rt[s] = router[...]
    tmp[...] = jnp.zeros_like(tmp)

    pl.semaphore_wait(barrier, 1 + (n_t - 1) + (n_dp - 1))

    pairs = [
        rcopy(ref, ref, pair_s.at[i], pair_r.at[i], (d, t, other))
        for i, ref in enumerate((xtok.at[s], rt.at[s], gn.at[s]))
    ]
    for c in pairs:
        c.start()
        later(c.wait_send)

    last_hop = gather_hops
    far_targets = [t_peer(n_t // 2), t_peer((n_t - last_hop) + s * (2 * last_hop - n_t))]
    fars = [
        rcopy(xg, far.at[j, s], far_s.at[j], far_r.at[j], (d, p, s)) for j, p in enumerate(far_targets)
    ]
    for c in fars:
        c.start()
        later(c.wait_send)

    def wd_send(i, carry):
        p = t_peer(i)
        rcopy(w_down.at[0, :, down_cols(p)], wdb.at[t], wd_s, wd_r, (d, p, s)).start()
        return carry

    lax.fori_loop(1, n_t, wd_send, 0)
    later(wait_bytes, wdb.at[pl.ds(0, n_t - 1)], wd_s)

    def pack(value_of, g, dst):
        s0, ns = groups[g]
        pr = plane_rows(ns, chunks)
        for c in range(chunks):
            v = value_of(c)
            for q in range(ns):
                tmp[pl.ds(c * ns + q, n_dp, stride=pr), :] = v[q * n_dp : (q + 1) * n_dp]
        dst[...] = tmp[: n_dp * pr].astype(BF).reshape(n_dp, pr, LANE)

    def exchange(src, dst, ssem, rsem):
        def one(i, carry):
            p = dp_peer(i)
            rcopy(src.at[p], dst.at[d], ssem, rsem, (p, t, s)).start()
            return carry

        lax.fori_loop(1, n_dp, one, 0)
        dst[d] = src[d]
        later(exchange_wait, src, ssem)

    def exchange_wait(dst, sem):
        wait_bytes(dst.at[pl.ds(0, n_dp - 1)], sem)

    def dispatch(j, sources):
        for g, (s0, ns) in enumerate(groups):
            sel = chosen[s0 * n_dp : (s0 + ns) * n_dp]
            halves = [dot(sel, src) for src in sources]
            k = j * ng + g
            pack(lambda c: halves[c // per_half][:, (c % per_half) * LANE : (c % per_half + 1) * LANE], g, send[k])
            exchange(send[k], recv[k], dis_s.at[k], dis_r.at[k])

    pairs[0].wait_recv()
    dispatch(0, [xtok[h] for h in range(2)])
    swaps = [rcopy(far.at[j, s], far.at[j, s], far_s.at[2 + j], far_r.at[2 + j], (d, t, other)) for j in range(2)]
    for j in range(2):
        fars[j].wait_recv()
        swaps[j].start()
        later(swaps[j].wait_send)
    for j in range(2):
        swaps[j].wait_recv()
        dispatch(1 + j, [far[j, h] for h in range(2)])

    for c in pairs[1:]:
        c.wait_recv()
    part = jnp.zeros((toks, experts), F32)
    sq = jnp.zeros((toks, 1), F32)
    for h in range(2):
        xf = xtok[h].astype(F32)
        sq = sq + jnp.sum(xf * xf, axis=1, keepdims=True)
        part = part + dot(xf * gn[h][0:1], rt[h].astype(F32), precision=HIGH)
    for j in range(n_t):
        lp[j, 0] = part[j * piece : (j + 1) * piece]
        lp[j, 1] = jnp.broadcast_to(sq[j * piece : (j + 1) * piece], (piece, experts))

    def lp_send(i, carry):
        p = t_peer(i)
        rcopy(lp.at[p], lr.at[t], lp_s, lp_r, (d, p, s)).start()
        return carry

    lax.fori_loop(1, n_t, lp_send, 0)
    later(wait_bytes, lr.at[pl.ds(0, n_t - 1)], lp_s)
    lr[t] = lp[t]
    wait_bytes(lr.at[pl.ds(0, n_t - 1)], lp_r)
    tot = lr[0]
    for j in range(1, n_t):
        tot = tot + lr[j]
    lg[t] = tot[0] * lax.rsqrt(tot[1] / width + 1e-06)

    def lg_send(i, carry):
        rcopy(lg.at[t], lg.at[t], lg_s, lg_r, (d, t_peer(i), s)).start()
        return carry

    lax.fori_loop(1, n_t, lg_send, 0)
    later(wait_bytes, lg.at[pl.ds(0, n_t - 1)], lg_s)

    r_of = lax.broadcasted_iota(jnp.int32, (experts, rows), 1)
    expand_t = jnp.where(
        lax.broadcasted_iota(jnp.int32, (experts, rows), 0) == 2 * (r_of % n_dp) + s, 1.0, 0.0
    ).astype(BF)
    slot_of = lax.broadcasted_iota(jnp.int32, (toks, rows), 1) // n_dp + 1
    mine = dot(taken, expand_t, TN) == slot_of.astype(F32)
    wait_bytes(lg.at[pl.ds(0, n_t - 1)], lg_r)
    logits = jnp.concatenate([lg[j] for j in range(n_t)], axis=0).T
    masked = jnp.where(onehot > 0.0, logits, -jnp.inf)
    ex = jnp.exp(masked - jnp.max(masked, axis=0, keepdims=True))
    weights = ex / jnp.sum(ex, axis=0, keepdims=True)
    w_hi = weights.astype(BF)
    w_lo = (weights - w_hi.astype(F32)).astype(BF)
    ct[0] = jnp.where(mine, dot(w_hi, expand_t, TN), 0.0).astype(BF)
    ct[1] = jnp.where(mine, dot(w_lo, expand_t, TN), 0.0).astype(BF)
    wait_bytes(wt, wt_r)
    own_down.wait()

    right, left = t_peer(1), t_peer(n_t - 1)
    hops = gather_hops

    def ring(g, hop, direction, h, incoming):
        step = hop if incoming else hop - 1
        origin = t_peer((n_t - step) % n_t) if direction == 0 else t_peer(step)
        ref = ag[g].at[origin, h]
        k = (direction * hops + hop - 1) * 2 + h
        return origin, rcopy(
            ref, ref, ag_s.at[g, k], ag_r.at[g, k], (d, right if direction == 0 else left, s)
        )

    def ring_start(g, hop, direction, h):
        c = ring(g, hop, direction, h, False)[1]
        c.start()
        later(c.wait_send)

    def legs(hop):
        if hop < hops:
            return [(h, direction) for h in range(2) for direction in range(2)]
        return [(0, 0), (1, 1)]

    def unpack(src, g, use):
        s0, ns = groups[g]
        pr = plane_rows(ns, chunks)
        tmp[: n_dp * pr] = src[...].astype(F32).reshape(n_dp * pr, LANE)
        for q in range(ns):
            use(q, [tmp[pl.ds(c * ns + q, n_dp, stride=pr), :] for c in range(chunks)])

    def do_rows(g):
        s0, ns = groups[g]
        exchange_wait(recv[g], dis_r.at[g])
        squares = []

        def scale(q, cols):
            squares.append(sum(v * v for v in cols))
            for c, v in enumerate(cols):
                h, l0 = c // per_half, (c % per_half) * LANE
                ag[g][t, h, q * n_dp : (q + 1) * n_dp, l0 : l0 + LANE] = (v * gn[h][0:1, l0 : l0 + LANE]).astype(BF)

        unpack(recv[g], g, scale)
        for h, direction in legs(1):
            ring_start(g, 1, direction, h)
        ones = jnp.ones((8, LANE), F32)
        cols = pl.ds(s0 * n_dp, ns * n_dp)
        for q in range(ns):
            ss[t, :, (s0 + q) * n_dp : (s0 + q + 1) * n_dp] = dot(ones, squares[q], NT, precision=HIGH)

        def ss_send(i, carry):
            rcopy(ss.at[t, :, cols], ss.at[t, :, cols], ss_s.at[g], ss_r.at[g], (d, t_peer(i), s)).start()
            return carry

        lax.fori_loop(1, n_t, ss_send, 0)
        later(wait_bytes, ss.at[pl.ds(0, n_t - 1), :, cols], ss_s.at[g])
        acc[g][...] = dot(wt[t, 0], ag[g][t, 0], NT) + dot(wt[t, 1], ag[g][t, 1], NT)

    def do_far(g, j):
        k = (1 + j) * ng + g
        exchange_wait(recv[k], dis_r.at[k])
        origins = [t_peer(n_t // 2)] * 2 if j == 0 else [t_peer(last_hop), t_peer(n_t - last_hop)]

        def keep(q, cols):
            for c, v in enumerate(cols):
                h, l0 = c // per_half, (c % per_half) * LANE
                ag[g][origins[h], h, q * n_dp : (q + 1) * n_dp, l0 : l0 + LANE] = v.astype(BF)

        unpack(recv[k], g, keep)
        for h, o in enumerate(origins):
            acc[g][...] += dot(wt[o, h], ag[g][o, h], NT)

    def do_gather(g, hop):
        going = legs(hop + 1) if hop < hops else []
        for h, direction in legs(hop):
            origin, c = ring(g, hop, direction, h, True)
            c.wait_recv()
            if (h, direction) in going:
                ring_start(g, hop + 1, direction, h)
            acc[g][...] += dot(wt[origin, h], ag[g][origin, h], NT)

    half = hid_n // 2

    def unit_legs(hop):
        if hop < unit_hops:
            return [(h, direction) for h in range(2) for direction in range(2)]
        return [(0, 0), (1, 1)]

    def units(g, hop, direction, h, incoming):
        step = hop if incoming else hop - 1
        origin = t_peer((n_t - step) % n_t) if direction == 0 else t_peer(step)
        ref = hid[g].at[origin, pl.ds(h * half, half)]
        k = (direction * unit_hops + hop - 1) * 2 + h
        return origin, rcopy(
            ref, ref, hid_s.at[g, k], hid_r.at[g, k], (d, right if direction == 0 else left, s)
        )

    def units_start(g, hop, direction, h):
        c = units(g, hop, direction, h, False)[1]
        c.start()
        later(c.wait_send)

    def do_hidden(g):
        s0, ns = groups[g]
        cols = slice(s0 * n_dp, (s0 + ns) * n_dp)
        wait_bytes(ss.at[pl.ds(0, n_t - 1), :, pl.ds(s0 * n_dp, ns * n_dp)], ss_r.at[g])
        total = ss[0, 0:1, cols]
        for j in range(1, n_t):
            total = total + ss[j, 0:1, cols]
        rinv = lax.rsqrt(total / width + 1e-06)
        gate = acc[g][0:hid_n] * rinv
        hid[g][t] = (gate * jax.nn.sigmoid(gate) * (acc[g][hid_n : 2 * hid_n] * rinv)).astype(BF)
        for h, direction in unit_legs(1):
            units_start(g, 1, direction, h)
        if g == 0:
            wait_bytes(wdb.at[pl.ds(0, n_t - 1)], wd_r)
        oacc[g][...] = dot(hid[g][t], wdb[t], TN)

    def do_units(g, hop):
        got = [None, None]
        going = unit_legs(hop + 1) if hop < unit_hops else []
        for h, direction in unit_legs(hop):
            origin, c = units(g, hop, direction, h, True)
            c.wait_recv()
            got[direction] = origin
            if (h, direction) in going:
                units_start(g, hop + 1, direction, h)
        for origin in got if hop < unit_hops else got[:1]:
            oacc[g][...] += dot(hid[g][origin], wdb[origin], TN)

    def do_back(g):
        pack(lambda c: oacc[g][:, c * LANE : (c + 1) * LANE], g, send2[g])
        exchange(send2[g], recv2[g], ret_s.at[g], ret_r.at[g])

    does = {"rows": do_rows, "far": do_far, "gather": do_gather, "hidden": do_hidden, "units": do_units, "back": do_back}
    for name, *args in schedule(ng, gather_hops, unit_hops):
        does[name](*args)

    for g, (s0, ns) in enumerate(groups):
        exchange_wait(recv2[g], ret_r.at[g])

        def keep(q, cols):
            for c, v in enumerate(cols):
                oacc[g][q * n_dp : (q + 1) * n_dp, c * LANE : (c + 1) * LANE] = v

        unpack(recv2[g], g, keep)
        for h in range(2):
            z = oacc[g][:, h * feats : (h + 1) * feats].astype(BF)
            cols = slice(s0 * n_dp, (s0 + ns) * n_dp)
            m = dot(ct[0, :, cols], z) + dot(ct[1, :, cols], z)
            mixs[h] = m if g == 0 else mixs[h] + m
    last = rcopy(mixs.at[other], mixr, mix_s, mix_r, (d, t, other))
    last.start()
    last.wait_recv()
    out[...] = (mixs[s] + mixr[...]).astype(BF)
    later(last.wait_send)

    for f in left_over:
        f()


def body(tokens, gain, router, routes, w_gate, w_up, w_down):
    toks, feats = tokens.shape
    top = routes.shape[1]
    n_dp, n_t, n_side = (lax.axis_size(a) for a in ("dp", "tensor", "side"))
    experts = n_dp * n_side
    slots = min(toks, max(2, toks * top * 5 // (experts * 4)))
    hid_n = w_gate.shape[2]
    groups = split_slots(slots)
    chunks = 2 * feats // LANE
    n_rows = [ns * n_dp for _, ns in groups]
    planes = [plane_rows(ns, chunks) for _, ns in groups]
    rows = slots * n_dp
    gather_hops, unit_hops = n_t // 2 - 1, n_t // 2
    piece = toks // n_t
    cfg = (n_dp, n_t, slots, groups, toks, feats, experts, top, hid_n)
    vm = pltpu.VMEM
    dma = pltpu.SemaphoreType.DMA
    ng = len(groups)
    plane_bufs = [vm((n_dp, p, LANE), BF) for p in planes]
    scratch = (
        [
            vm((2, toks, feats), BF),
            vm((toks, feats), BF),
            vm((2, 2, toks, feats), BF),
            vm((2, feats, experts), BF),
            vm((2, 8, feats), F32),
            vm((rows, toks), BF),
            vm((n_dp * max(planes), LANE), F32),
            vm((n_t, 2, piece, experts), F32),
            vm((n_t, 2, piece, experts), F32),
            vm((n_t, piece, experts), F32),
            vm((n_t, 8, rows), F32),
            vm((n_t, 2, 2 * hid_n, feats), BF),
            vm((n_t, hid_n, 2 * feats), BF),
            vm((2, toks, rows), BF),
            vm((2, toks, feats), F32),
            vm((toks, feats), F32),
        ]
        + plane_bufs * 8
        + [vm((n_t, 2, n, feats), BF) for n in n_rows]
        + [vm((n_t, hid_n, n), BF) for n in n_rows]
        + [vm((2 * hid_n, n), F32) for n in n_rows]
        + [vm((n, 2 * feats), F32) for n in n_rows]
        + [dma((3,)), dma((3,)), dma((4,)), dma((4,))]
        + [dma] * 10
        + [dma((3 * ng,))] * 2
        + [dma((ng,))] * 4
        + [dma((ng, 4 * gather_hops))] * 2
        + [dma((ng, 4 * unit_hops))] * 2
    )
    in_vmem, in_hbm = pl.BlockSpec(memory_space=vm), pl.BlockSpec(memory_space=pl.ANY)
    return pl.pallas_call(
        functools.partial(kernel, cfg),
        out_shape=jax.ShapeDtypeStruct((toks, feats), BF),
        in_specs=[in_vmem] * 4 + [in_hbm] * 3,
        out_specs=in_vmem,
        scratch_shapes=scratch,
        compiler_params=pltpu.CompilerParams(
            collective_id=0, has_side_effects=True, vmem_limit_bytes=56 * 1024 * 1024
        ),
        name="routed_experts",
    )(
        tokens,
        gain,
        router,
        routes.T,
        jnp.swapaxes(w_gate, 1, 2),
        jnp.swapaxes(w_up, 1, 2),
        w_down,
    )


def solution(mesh):
    placed = (
        P("dp", ("tensor", "side")),
        P(("tensor", "side")),
        P(("tensor", "side"), None),
        P("dp", None),
        P(("dp", "side"), None, "tensor"),
        P(("dp", "side"), None, "tensor"),
        P(("dp", "side"), "tensor", None),
    )
    return jax.shard_map(
        body, mesh=mesh, in_specs=placed, out_specs=P("dp", ("tensor", "side")), check_vma=False
    )
```

```python
import functools

import jax
import jax.numpy as jnp
from jax import lax
from jax.experimental import pallas as pl
from jax.experimental.pallas import tpu as pltpu
from jax.sharding import PartitionSpec as P

MESH = pl.DeviceIdType.MESH
BF = jnp.bfloat16
F32 = jnp.float32
LANE = 128
HIGH = lax.Precision.HIGHEST
NT = (((1,), (1,)), ((), ()))
TN = (((0,), (0,)), ((), ()))


def dot(a, b, dims=(((1,), (0,)), ((), ())), precision=None):
    return lax.dot_general(a, b, dims, precision=precision, preferred_element_type=F32)


def split_slots(slots):
    return ((0, slots - 2), (slots - 2, 2))


def plane_rows(count, chunks):
    return -(-count * chunks // 8) * 8


def schedule(ng, gather_hops, unit_hops):
    steps = [("farsend", 0), ("rows",), ("farsend", 1), ("logits",)]
    for k in range(1, gather_hops):
        steps += [("gather", g, k) for g in range(ng)]
    steps += [("weights",), ("far", 0), ("far", 1)]
    for g in range(ng):
        steps += [("gather", g, gather_hops), ("hidden", g)]
    for k in range(1, unit_hops + 1):
        for g in range(ng):
            steps += [("units", g, k)] + ([("back", g)] if k == unit_hops else [])
    return steps


def kernel(cfg, *refs):
    n_dp, n_t, slots, groups, toks, feats, experts, top, hid_n = cfg
    it = iter(refs)
    take = lambda n: [next(it) for _ in range(n)]
    tokens, gain, router, routes, w_gate, w_up, w_down, out = take(8)
    xtok, xg, far, stage_x, stage_w, rt, gn, chosen, tmp, lp, lr, lg, ss, wt, wdb, ct, mixs, mixr = take(18)
    ng = len(groups)
    send, recv = take(3), take(3)
    send2, recv2, hid, oacc, ag, acc = [take(ng) for _ in range(6)]
    pair_s, pair_r, far_s, far_r, wd_s, wd_r, lp_s, lp_r, lg_s, lg_r, mix_s, mix_r, wt_r, wl_r = take(14)
    dis_s, dis_r, ret_s, ret_r, ss_s, ss_r, ag_s, ag_r, hid_s, hid_r = take(10)

    d, t, s = lax.axis_index("dp"), lax.axis_index("tensor"), lax.axis_index("side")
    nz = 8 if n_dp % 8 == 0 else n_dp
    nx = n_dp // nz
    chunks = 2 * feats // LANE
    per_half = feats // LANE
    piece = toks // n_t
    width = 2 * feats * n_t
    rows = slots * n_dp
    other = 1 - s
    gather_hops, unit_hops = n_t // 2 - 1, n_t // 2
    left_over = []

    def dp_peer(i):
        return lax.rem(d // nz + i // nz, nx) * nz + lax.rem(d % nz + i % nz, nz)

    def t_peer(i):
        return lax.rem(t + i, n_t)

    def rcopy(src, dst, ssem, rsem, dev):
        return pltpu.make_async_remote_copy(
            src_ref=src, dst_ref=dst, send_sem=ssem, recv_sem=rsem, device_id=dev, device_id_type=MESH
        )

    def wait_bytes(ref, sem):
        pltpu.make_async_copy(ref, ref, sem).wait()

    def later(f, *args):
        left_over.append(lambda: f(*args))

    barrier = pltpu.get_barrier_semaphore()
    pl.semaphore_signal(barrier, inc=1, device_id=(d, t, other), device_id_type=MESH)

    def greet_t(i, carry):
        pl.semaphore_signal(barrier, inc=1, device_id=(d, t_peer(i), s), device_id_type=MESH)
        return carry

    def greet_dp(i, carry):
        pl.semaphore_signal(barrier, inc=1, device_id=(dp_peer(i), t, s), device_id_type=MESH)
        return carry

    lax.fori_loop(1, n_t, greet_t, 0)
    lax.fori_loop(1, n_dp, greet_dp, 0)

    def weights_in(j, carry):
        for h in range(2):
            k0 = pl.ds(pl.multiple_of(j * 2 * feats + h * feats, feats), feats)
            pltpu.make_async_copy(w_gate.at[0, :, k0], wt.at[j, h, pl.ds(0, hid_n)], wt_r).start()
            pltpu.make_async_copy(w_up.at[0, :, k0], wt.at[j, h, pl.ds(hid_n, hid_n)], wt_r).start()
        return carry

    lax.fori_loop(0, n_t, weights_in, 0)
    down_cols = lambda p: pl.ds(pl.multiple_of(p * 2 * feats, 2 * feats), 2 * feats)
    own_down = pltpu.make_async_copy(w_down.at[0, :, down_cols(t)], wdb.at[t], wl_r)
    own_down.start()

    gn[s] = jnp.broadcast_to(gain[...].astype(F32), (8, feats))
    xtok[s] = tokens[...]
    xg[...] = (tokens[...].astype(F32) * gn[s, 0:1]).astype(BF)
    rt[s] = router[...]
    tmp[...] = jnp.zeros_like(tmp)

    pl.semaphore_wait(barrier, 1 + (n_t - 1) + (n_dp - 1))

    pairs = [
        rcopy(ref, ref, pair_s.at[i], pair_r.at[i], (d, t, other))
        for i, ref in enumerate((xtok.at[s], rt.at[s], gn.at[s]))
    ]
    for c in pairs:
        c.start()
        later(c.wait_send)

    half_way = n_t // 2
    near = (d, t_peer(1 + s * (n_t - 2)), s)
    onward = (d, t_peer(gather_hops + s * (n_t - 2 * gather_hops)), s)
    staged_x = rcopy(xg, stage_x, far_s.at[0], far_r.at[0], near)
    staged_w = rcopy(w_down.at[0, :, down_cols(t_peer(half_way))], stage_w, far_s.at[1], far_r.at[1], near)
    b_peer = t_peer((n_t - gather_hops) + s * (2 * gather_hops - n_t))
    far_b = rcopy(xg, far.at[1, s], far_s.at[2], far_r.at[2], (d, b_peer, s))
    for c in (staged_x, far_b, staged_w):
        c.start()
        later(c.wait_send)

    def wd_send(i, carry):
        p = t_peer(i)
        rcopy(w_down.at[0, :, down_cols(p)], wdb.at[t], wd_s, wd_r, (d, p, s)).start()
        return carry

    lax.fori_loop(1, half_way, wd_send, 0)
    lax.fori_loop(half_way + 1, n_t, wd_send, 0)
    later(wait_bytes, wdb.at[pl.ds(0, n_t - 2)], wd_s)

    e_ids = lax.broadcasted_iota(jnp.int32, (experts, toks), 0)
    routes_v = routes[...]
    onehot = jnp.zeros((experts, toks), F32)
    for k in range(top):
        onehot = onehot + jnp.where(routes_v[k : k + 1, :] == e_ids, 1.0, 0.0)
    earlier = jnp.where(
        lax.broadcasted_iota(jnp.int32, (toks, toks), 0) < lax.broadcasted_iota(jnp.int32, (toks, toks), 1), 1.0, 0.0
    )
    before = dot(onehot.astype(BF), earlier.astype(BF))
    taken = (onehot * (before + 1.0)).astype(BF)

    r_of = lax.broadcasted_iota(jnp.int32, (rows, experts), 0)
    expand = jnp.where(
        lax.broadcasted_iota(jnp.int32, (rows, experts), 1) == 2 * (r_of % n_dp) + s, 1.0, 0.0
    ).astype(BF)
    slot_of = lax.broadcasted_iota(jnp.int32, (rows, toks), 0) // n_dp + 1
    chosen[...] = jnp.where(dot(expand, taken) == slot_of.astype(F32), 1.0, 0.0).astype(BF)
    def pack(value_of, ns, dst):
        pr = plane_rows(ns, chunks)
        for c in range(chunks):
            v = value_of(c)
            for q in range(ns):
                tmp[pl.ds(c * ns + q, n_dp, stride=pr), :] = v[q * n_dp : (q + 1) * n_dp]
        dst[...] = tmp[: n_dp * pr].astype(BF).reshape(n_dp, pr, LANE)

    def exchange(src, dst, ssem, rsem):
        def one(i, carry):
            p = dp_peer(i)
            rcopy(src.at[p], dst.at[d], ssem, rsem, (p, t, s)).start()
            return carry

        lax.fori_loop(1, n_dp, one, 0)
        dst[d] = src[d]
        later(exchange_wait, src, ssem)

    def exchange_wait(dst, sem):
        wait_bytes(dst.at[pl.ds(0, n_dp - 1)], sem)

    def dispatch(j, sources):
        halves = [dot(chosen[...], src) for src in sources]
        pack(
            lambda c: halves[c // per_half][:, (c % per_half) * LANE : (c % per_half + 1) * LANE], slots, send[j]
        )
        exchange(send[j], recv[j], dis_s.at[j], dis_r.at[j])

    pairs[0].wait_recv()
    dispatch(0, [xtok[h] for h in range(2)])

    staged_x.wait_recv()
    far_a = rcopy(stage_x, far.at[0, s], far_s.at[3], far_r.at[3], onward)
    far_a.start()
    later(far_a.wait_send)
    staged_w.wait_recv()
    origin_w = t_peer((n_t - 1) - s * (n_t - 2))
    pass_w = rcopy(stage_w, wdb.at[origin_w], far_s.at[4], wd_r, onward)
    pass_w.start()
    later(pass_w.wait_send)
    swaps = [rcopy(far.at[j, s], far.at[j, s], far_s.at[5 + j], far_r.at[5 + j], (d, t, other)) for j in range(2)]
    for j, c in ((1, far_b), (0, far_a)):
        c.wait_recv()
        swaps[j].start()
        later(swaps[j].wait_send)

    for c in pairs[1:]:
        c.wait_recv()
    part = jnp.zeros((toks, experts), F32)
    sq = jnp.zeros((toks, 1), F32)
    for h in range(2):
        xf = xtok[h].astype(F32)
        sq = sq + jnp.sum(xf * xf, axis=1, keepdims=True)
        part = part + dot(xf * gn[h][0:1], rt[h].astype(F32), precision=HIGH)
    for j in range(n_t):
        lp[j, 0] = part[j * piece : (j + 1) * piece]
        lp[j, 1] = jnp.broadcast_to(sq[j * piece : (j + 1) * piece], (piece, experts))

    def lp_send(i, carry):
        p = t_peer(i)
        rcopy(lp.at[p], lr.at[t], lp_s, lp_r, (d, p, s)).start()
        return carry

    lax.fori_loop(1, n_t, lp_send, 0)
    later(wait_bytes, lr.at[pl.ds(0, n_t - 1)], lp_s)
    lr[t] = lp[t]
    wait_bytes(wt, wt_r)
    own_down.wait()

    right, left = t_peer(1), t_peer(n_t - 1)
    hops = gather_hops

    def ring(g, hop, direction, h, incoming):
        step = hop if incoming else hop - 1
        origin = t_peer((n_t - step) % n_t) if direction == 0 else t_peer(step)
        ref = ag[g].at[origin, h]
        k = (direction * hops + hop - 1) * 2 + h
        return origin, rcopy(
            ref, ref, ag_s.at[g, k], ag_r.at[g, k], (d, right if direction == 0 else left, s)
        )

    def ring_start(g, hop, direction, h):
        c = ring(g, hop, direction, h, False)[1]
        c.start()
        later(c.wait_send)

    def legs(hop):
        if hop < hops:
            return [(h, direction) for h in range(2) for direction in range(2)]
        return [(0, 0), (1, 1)]

    def unpack(src, ns, use):
        pr = plane_rows(ns, chunks)
        tmp[: n_dp * pr] = src[...].astype(F32).reshape(n_dp * pr, LANE)
        for q in range(ns):
            use(q, [tmp[pl.ds(c * ns + q, n_dp, stride=pr), :] for c in range(chunks)])

    def group_of(q):
        for g, (s0, ns) in enumerate(groups):
            if s0 <= q < s0 + ns:
                return g, slice((q - s0) * n_dp, (q - s0 + 1) * n_dp)

    def do_rows():
        exchange_wait(recv[0], dis_r.at[0])
        squares = []

        def scale(q, cols):
            squares.append(sum(v * v for v in cols))
            g, at = group_of(q)
            for c, v in enumerate(cols):
                h, l0 = c // per_half, (c % per_half) * LANE
                ag[g][t, h, at, l0 : l0 + LANE] = (v * gn[h][0:1, l0 : l0 + LANE]).astype(BF)

        unpack(recv[0], slots, scale)
        for g in range(ng):
            for h, direction in legs(1):
                ring_start(g, 1, direction, h)
        ones = jnp.ones((8, LANE), F32)
        for q in range(slots):
            ss[t, :, q * n_dp : (q + 1) * n_dp] = dot(ones, squares[q], NT, precision=HIGH)

        def ss_send(i, carry):
            rcopy(ss.at[t], ss.at[t], ss_s, ss_r, (d, t_peer(i), s)).start()
            return carry

        lax.fori_loop(1, n_t, ss_send, 0)
        later(wait_bytes, ss.at[pl.ds(0, n_t - 1)], ss_s)
        for g in range(ng):
            acc[g][...] = dot(wt[t, 0], ag[g][t, 0], NT) + dot(wt[t, 1], ag[g][t, 1], NT)

    def do_farsend(j):
        swaps[j].wait_recv()
        dispatch(1 + j, [far[j, h] for h in range(2)])

    def do_far(j):
        exchange_wait(recv[1 + j], dis_r.at[1 + j])
        origins = [t_peer(half_way)] * 2 if j == 0 else [t_peer(gather_hops), t_peer(n_t - gather_hops)]

        def keep(q, cols):
            g, at = group_of(q)
            for c, v in enumerate(cols):
                h, l0 = c // per_half, (c % per_half) * LANE
                ag[g][origins[h], h, at, l0 : l0 + LANE] = v.astype(BF)

        unpack(recv[1 + j], slots, keep)
        for g in range(ng):
            for h, o in enumerate(origins):
                acc[g][...] += dot(wt[o, h], ag[g][o, h], NT)

    def do_gather(g, hop):
        going = legs(hop + 1) if hop < hops else []
        for h, direction in legs(hop):
            origin, c = ring(g, hop, direction, h, True)
            c.wait_recv()
            if (h, direction) in going:
                ring_start(g, hop + 1, direction, h)
            acc[g][...] += dot(wt[origin, h], ag[g][origin, h], NT)

    half = hid_n // 2

    def unit_legs(hop):
        if hop < unit_hops:
            return [(h, direction) for h in range(2) for direction in range(2)]
        return [(0, 0), (1, 1)]

    def units(g, hop, direction, h, incoming):
        step = hop if incoming else hop - 1
        origin = t_peer((n_t - step) % n_t) if direction == 0 else t_peer(step)
        ref = hid[g].at[origin, pl.ds(h * half, half)]
        k = (direction * unit_hops + hop - 1) * 2 + h
        return origin, rcopy(
            ref, ref, hid_s.at[g, k], hid_r.at[g, k], (d, right if direction == 0 else left, s)
        )

    def units_start(g, hop, direction, h):
        c = units(g, hop, direction, h, False)[1]
        c.start()
        later(c.wait_send)

    def do_hidden(g):
        s0, ns = groups[g]
        cols = slice(s0 * n_dp, (s0 + ns) * n_dp)
        if g == 0:
            wait_bytes(ss.at[pl.ds(0, n_t - 1)], ss_r)
        total = ss[0, 0:1, cols]
        for j in range(1, n_t):
            total = total + ss[j, 0:1, cols]
        rinv = lax.rsqrt(total / width + 1e-06)
        gate = acc[g][0:hid_n] * rinv
        hid[g][t] = (gate * jax.nn.sigmoid(gate) * (acc[g][hid_n : 2 * hid_n] * rinv)).astype(BF)
        for h, direction in unit_legs(1):
            units_start(g, 1, direction, h)
        if g == 0:
            wait_bytes(wdb.at[pl.ds(0, n_t - 1)], wd_r)
        oacc[g][...] = dot(hid[g][t], wdb[t], TN)

    def do_units(g, hop):
        got = [None, None]
        going = unit_legs(hop + 1) if hop < unit_hops else []
        for h, direction in unit_legs(hop):
            origin, c = units(g, hop, direction, h, True)
            c.wait_recv()
            got[direction] = origin
            if (h, direction) in going:
                units_start(g, hop + 1, direction, h)
        for origin in got if hop < unit_hops else got[:1]:
            oacc[g][...] += dot(hid[g][origin], wdb[origin], TN)

    def do_back(g):
        pack(lambda c: oacc[g][:, c * LANE : (c + 1) * LANE], groups[g][1], send2[g])
        exchange(send2[g], recv2[g], ret_s.at[g], ret_r.at[g])

    def do_logits():
        wait_bytes(lr.at[pl.ds(0, n_t - 1)], lp_r)
        tot = lr[0]
        for j in range(1, n_t):
            tot = tot + lr[j]
        lg[t] = tot[0] * lax.rsqrt(tot[1] / width + 1e-06)

        def lg_send(i, carry):
            rcopy(lg.at[t], lg.at[t], lg_s, lg_r, (d, t_peer(i), s)).start()
            return carry

        lax.fori_loop(1, n_t, lg_send, 0)
        later(wait_bytes, lg.at[pl.ds(0, n_t - 1)], lg_s)

    def do_weights():
        r_of = lax.broadcasted_iota(jnp.int32, (experts, rows), 1)
        expand_t = jnp.where(
            lax.broadcasted_iota(jnp.int32, (experts, rows), 0) == 2 * (r_of % n_dp) + s, 1.0, 0.0
        ).astype(BF)
        slot_of = lax.broadcasted_iota(jnp.int32, (toks, rows), 1) // n_dp + 1
        mine = dot(taken, expand_t, TN) == slot_of.astype(F32)
        wait_bytes(lg.at[pl.ds(0, n_t - 1)], lg_r)
        logits = jnp.concatenate([lg[j] for j in range(n_t)], axis=0).T
        masked = jnp.where(onehot > 0.0, logits, -jnp.inf)
        ex = jnp.exp(masked - jnp.max(masked, axis=0, keepdims=True))
        weights = ex / jnp.sum(ex, axis=0, keepdims=True)
        w_hi = weights.astype(BF)
        w_lo = (weights - w_hi.astype(F32)).astype(BF)
        ct[0] = jnp.where(mine, dot(w_hi, expand_t, TN), 0.0).astype(BF)
        ct[1] = jnp.where(mine, dot(w_lo, expand_t, TN), 0.0).astype(BF)

    does = {"logits": do_logits, "weights": do_weights, "rows": do_rows, "far": do_far, "farsend": do_farsend, "gather": do_gather, "hidden": do_hidden, "units": do_units, "back": do_back}
    for name, *args in schedule(ng, gather_hops, unit_hops):
        does[name](*args)

    for g, (s0, ns) in enumerate(groups):
        exchange_wait(recv2[g], ret_r.at[g])

        def keep(q, cols):
            for c, v in enumerate(cols):
                oacc[g][q * n_dp : (q + 1) * n_dp, c * LANE : (c + 1) * LANE] = v

        unpack(recv2[g], ns, keep)
        for h in range(2):
            z = oacc[g][:, h * feats : (h + 1) * feats].astype(BF)
            cols = slice(s0 * n_dp, (s0 + ns) * n_dp)
            m = dot(ct[0, :, cols], z) + dot(ct[1, :, cols], z)
            mixs[h] = m if g == 0 else mixs[h] + m
    last = rcopy(mixs.at[other], mixr, mix_s, mix_r, (d, t, other))
    last.start()
    last.wait_recv()
    out[...] = (mixs[s] + mixr[...]).astype(BF)
    later(last.wait_send)

    for f in left_over:
        f()


def body(tokens, gain, router, routes, w_gate, w_up, w_down):
    toks, feats = tokens.shape
    top = routes.shape[1]
    n_dp, n_t, n_side = (lax.axis_size(a) for a in ("dp", "tensor", "side"))
    experts = n_dp * n_side
    slots = min(toks, max(2, toks * top * 5 // (experts * 4)))
    hid_n = w_gate.shape[2]
    groups = split_slots(slots)
    chunks = 2 * feats // LANE
    n_rows = [ns * n_dp for _, ns in groups]
    planes = [plane_rows(ns, chunks) for _, ns in groups]
    plane = plane_rows(slots, chunks)
    rows = slots * n_dp
    gather_hops, unit_hops = n_t // 2 - 1, n_t // 2
    piece = toks // n_t
    cfg = (n_dp, n_t, slots, groups, toks, feats, experts, top, hid_n)
    vm = pltpu.VMEM
    dma = pltpu.SemaphoreType.DMA
    ng = len(groups)
    plane_bufs = [vm((n_dp, p, LANE), BF) for p in planes]
    scratch = (
        [
            vm((2, toks, feats), BF),
            vm((toks, feats), BF),
            vm((2, 2, toks, feats), BF),
            vm((toks, feats), BF),
            vm((hid_n, 2 * feats), BF),
            vm((2, feats, experts), BF),
            vm((2, 8, feats), F32),
            vm((rows, toks), BF),
            vm((n_dp * plane, LANE), F32),
            vm((n_t, 2, piece, experts), F32),
            vm((n_t, 2, piece, experts), F32),
            vm((n_t, piece, experts), F32),
            vm((n_t, 8, rows), F32),
            vm((n_t, 2, 2 * hid_n, feats), BF),
            vm((n_t, hid_n, 2 * feats), BF),
            vm((2, toks, rows), BF),
            vm((2, toks, feats), F32),
            vm((toks, feats), F32),
        ]
        + [vm((n_dp, plane, LANE), BF)] * 6
        + plane_bufs * 2
        + [vm((n_t, hid_n, n), BF) for n in n_rows]
        + [vm((n, 2 * feats), F32) for n in n_rows]
        + [vm((n_t, 2, n, feats), BF) for n in n_rows]
        + [vm((2 * hid_n, n), F32) for n in n_rows]
        + [dma((3,)), dma((3,)), dma((7,)), dma((7,))]
        + [dma] * 10
        + [dma((3,))] * 2
        + [dma((ng,))] * 2
        + [dma] * 2
        + [dma((ng, 4 * gather_hops))] * 2
        + [dma((ng, 4 * unit_hops))] * 2
    )
    in_vmem, in_hbm = pl.BlockSpec(memory_space=vm), pl.BlockSpec(memory_space=pl.ANY)
    return pl.pallas_call(
        functools.partial(kernel, cfg),
        out_shape=jax.ShapeDtypeStruct((toks, feats), BF),
        in_specs=[in_vmem] * 4 + [in_hbm] * 3,
        out_specs=in_vmem,
        scratch_shapes=scratch,
        compiler_params=pltpu.CompilerParams(
            collective_id=0, has_side_effects=True, vmem_limit_bytes=56 * 1024 * 1024
        ),
        name="routed_experts",
    )(
        tokens,
        gain,
        router,
        routes.T,
        jnp.swapaxes(w_gate, 1, 2),
        jnp.swapaxes(w_up, 1, 2),
        w_down,
    )


def solution(mesh):
    placed = (
        P("dp", ("tensor", "side")),
        P(("tensor", "side")),
        P(("tensor", "side"), None),
        P("dp", None),
        P(("dp", "side"), None, "tensor"),
        P(("dp", "side"), None, "tensor"),
        P(("dp", "side"), "tensor", None),
    )
    return jax.shard_map(
        body, mesh=mesh, in_specs=placed, out_specs=P("dp", ("tensor", "side")), check_vma=False
    )
```

```python
import functools

import jax
import jax.numpy as jnp
from jax import lax
from jax.experimental import pallas as pl
from jax.experimental.pallas import tpu as pltpu
from jax.sharding import PartitionSpec as P

MESH = pl.DeviceIdType.MESH
BF = jnp.bfloat16
F32 = jnp.float32
LANE = 128
HIGH = lax.Precision.HIGHEST
NT = (((1,), (1,)), ((), ()))
TN = (((0,), (0,)), ((), ()))


def dot(a, b, dims=(((1,), (0,)), ((), ())), precision=None):
    return lax.dot_general(a, b, dims, precision=precision, preferred_element_type=F32)


def split_slots(slots):
    return ((0, slots - 2), (slots - 2, 2))


def plane_rows(count, chunks):
    return -(-count * chunks // 8) * 8


def schedule(ng, gather_hops, unit_hops):
    steps = [("farsend", 0), ("rows",), ("farsend", 1), ("logits",)]
    for k in range(1, gather_hops):
        steps += [("gather", g, k) for g in range(ng)]
        if k == 1:
            steps += [("far", 0)]
    steps += [("far", 1)] if gather_hops > 1 else [("far", 0), ("far", 1)]
    for g in range(ng):
        steps += [("gather", g, gather_hops), ("hidden", g)]
    for k in range(1, unit_hops + 1):
        for g in range(ng):
            steps += [("units", g, k)] + ([("back", g)] if k == unit_hops else [])
    return steps + [("weights",)]


def kernel(cfg, *refs):
    n_dp, n_t, slots, groups, toks, feats, experts, top, hid_n = cfg
    it = iter(refs)
    take = lambda n: [next(it) for _ in range(n)]
    tokens, gain, router, routes, w_gate, w_up, w_down, out = take(8)
    xtok, xg, far, stage_x, stage_w, rt, gn, chosen, tmp, lp, lr, lg, ss, wt, wdb, ct, mixs, mixr = take(18)
    ng = len(groups)
    send, recv = take(3), take(3)
    send2, recv2, hid, oacc, ag, acc = [take(ng) for _ in range(6)]
    pair_s, pair_r, far_s, far_r, wd_s, wd_r, lp_s, lp_r, lg_s, lg_r, mix_s, mix_r, wt_r, wl_r = take(14)
    dis_s, dis_r, ret_s, ret_r, ss_s, ss_r, ag_s, ag_r, hid_s, hid_r = take(10)

    d, t, s = lax.axis_index("dp"), lax.axis_index("tensor"), lax.axis_index("side")
    nz = 8 if n_dp % 8 == 0 else n_dp
    nx = n_dp // nz
    chunks = 2 * feats // LANE
    per_half = feats // LANE
    piece = toks // n_t
    width = 2 * feats * n_t
    rows = slots * n_dp
    other = 1 - s
    gather_hops, unit_hops = n_t // 2 - 1, n_t // 2
    left_over = []

    def dp_peer(i):
        return lax.rem(d // nz + i // nz, nx) * nz + lax.rem(d % nz + i % nz, nz)

    def t_peer(i):
        return lax.rem(t + i, n_t)

    def rcopy(src, dst, ssem, rsem, dev):
        return pltpu.make_async_remote_copy(
            src_ref=src, dst_ref=dst, send_sem=ssem, recv_sem=rsem, device_id=dev, device_id_type=MESH
        )

    def wait_bytes(ref, sem):
        pltpu.make_async_copy(ref, ref, sem).wait()

    def later(f, *args):
        left_over.append(lambda: f(*args))

    barrier = pltpu.get_barrier_semaphore()
    pl.semaphore_signal(barrier, inc=1, device_id=(d, t, other), device_id_type=MESH)

    def greet_t(i, carry):
        pl.semaphore_signal(barrier, inc=1, device_id=(d, t_peer(i), s), device_id_type=MESH)
        return carry

    def greet_dp(i, carry):
        pl.semaphore_signal(barrier, inc=1, device_id=(dp_peer(i), t, s), device_id_type=MESH)
        return carry

    lax.fori_loop(1, n_t, greet_t, 0)
    lax.fori_loop(1, n_dp, greet_dp, 0)

    def weights_in(j, carry):
        for h in range(2):
            k0 = pl.ds(pl.multiple_of(j * 2 * feats + h * feats, feats), feats)
            pltpu.make_async_copy(w_gate.at[0, :, k0], wt.at[j, h, pl.ds(0, hid_n)], wt_r).start()
            pltpu.make_async_copy(w_up.at[0, :, k0], wt.at[j, h, pl.ds(hid_n, hid_n)], wt_r).start()
        return carry

    lax.fori_loop(0, n_t, weights_in, 0)
    down_cols = lambda p: pl.ds(pl.multiple_of(p * 2 * feats, 2 * feats), 2 * feats)
    own_down = pltpu.make_async_copy(w_down.at[0, :, down_cols(t)], wdb.at[t], wl_r)
    own_down.start()

    gn[s] = jnp.broadcast_to(gain[...].astype(F32), (8, feats))
    xtok[s] = tokens[...]
    xg[...] = (tokens[...].astype(F32) * gn[s, 0:1]).astype(BF)
    rt[s] = router[...]
    tmp[...] = jnp.zeros_like(tmp)

    pl.semaphore_wait(barrier, 1 + (n_t - 1) + (n_dp - 1))

    pairs = [
        rcopy(ref, ref, pair_s.at[i], pair_r.at[i], (d, t, other))
        for i, ref in enumerate((xtok.at[s], rt.at[s], gn.at[s]))
    ]
    for c in pairs:
        c.start()
        later(c.wait_send)

    half_way = n_t // 2
    near = (d, t_peer(1 + s * (n_t - 2)), s)
    onward = (d, t_peer(gather_hops + s * (n_t - 2 * gather_hops)), s)
    staged_x = rcopy(xg, stage_x, far_s.at[0], far_r.at[0], near)
    staged_w = rcopy(w_down.at[0, :, down_cols(t_peer(half_way))], stage_w, far_s.at[1], far_r.at[1], near)
    b_peer = t_peer((n_t - gather_hops) + s * (2 * gather_hops - n_t))
    far_b = rcopy(xg, far.at[1, s], far_s.at[2], far_r.at[2], (d, b_peer, s))
    for c in (staged_x, far_b, staged_w):
        c.start()
        later(c.wait_send)

    def wd_send(i, carry):
        p = t_peer(i)
        rcopy(w_down.at[0, :, down_cols(p)], wdb.at[t], wd_s, wd_r, (d, p, s)).start()
        return carry

    lax.fori_loop(1, half_way, wd_send, 0)
    lax.fori_loop(half_way + 1, n_t, wd_send, 0)
    later(wait_bytes, wdb.at[pl.ds(0, n_t - 2)], wd_s)

    e_ids = lax.broadcasted_iota(jnp.int32, (experts, toks), 0)
    routes_v = routes[...]
    onehot = jnp.zeros((experts, toks), F32)
    for k in range(top):
        onehot = onehot + jnp.where(routes_v[k : k + 1, :] == e_ids, 1.0, 0.0)
    earlier = jnp.where(
        lax.broadcasted_iota(jnp.int32, (toks, toks), 0) < lax.broadcasted_iota(jnp.int32, (toks, toks), 1), 1.0, 0.0
    )
    before = dot(onehot.astype(BF), earlier.astype(BF))
    taken = (onehot * (before + 1.0)).astype(BF)

    r_of = lax.broadcasted_iota(jnp.int32, (rows, experts), 0)
    expand = jnp.where(
        lax.broadcasted_iota(jnp.int32, (rows, experts), 1) == 2 * (r_of % n_dp) + s, 1.0, 0.0
    ).astype(BF)
    slot_of = lax.broadcasted_iota(jnp.int32, (rows, toks), 0) // n_dp + 1
    chosen[...] = jnp.where(dot(expand, taken) == slot_of.astype(F32), 1.0, 0.0).astype(BF)
    def pack(value_of, ns, dst):
        pr = plane_rows(ns, chunks)
        for c in range(chunks):
            v = value_of(c)
            for q in range(ns):
                tmp[pl.ds(c * ns + q, n_dp, stride=pr), :] = v[q * n_dp : (q + 1) * n_dp]
        dst[...] = tmp[: n_dp * pr].astype(BF).reshape(n_dp, pr, LANE)

    def exchange(src, dst, ssem, rsem):
        def one(i, carry):
            p = dp_peer(i)
            rcopy(src.at[p], dst.at[d], ssem, rsem, (p, t, s)).start()
            return carry

        lax.fori_loop(1, n_dp, one, 0)
        dst[d] = src[d]
        later(exchange_wait, src, ssem)

    def exchange_wait(dst, sem):
        wait_bytes(dst.at[pl.ds(0, n_dp - 1)], sem)

    def dispatch(j, sources):
        halves = [dot(chosen[...], src) for src in sources]
        pack(
            lambda c: halves[c // per_half][:, (c % per_half) * LANE : (c % per_half + 1) * LANE], slots, send[j]
        )
        exchange(send[j], recv[j], dis_s.at[j], dis_r.at[j])

    pairs[0].wait_recv()
    dispatch(0, [xtok[h] for h in range(2)])

    staged_x.wait_recv()
    far_a = rcopy(stage_x, far.at[0, s], far_s.at[3], far_r.at[3], onward)
    far_a.start()
    later(far_a.wait_send)
    staged_w.wait_recv()
    origin_w = t_peer((n_t - 1) - s * (n_t - 2))
    pass_w = rcopy(stage_w, wdb.at[origin_w], far_s.at[4], wd_r, onward)
    pass_w.start()
    later(pass_w.wait_send)
    swaps = [rcopy(far.at[j, s], far.at[j, s], far_s.at[5 + j], far_r.at[5 + j], (d, t, other)) for j in range(2)]
    for j, c in ((1, far_b), (0, far_a)):
        c.wait_recv()
        swaps[j].start()
        later(swaps[j].wait_send)

    for c in pairs[1:]:
        c.wait_recv()
    part = jnp.zeros((toks, experts), F32)
    sq = jnp.zeros((toks, 1), F32)
    for h in range(2):
        xf = xtok[h].astype(F32)
        sq = sq + jnp.sum(xf * xf, axis=1, keepdims=True)
        part = part + dot(xf * gn[h][0:1], rt[h].astype(F32), precision=HIGH)
    for j in range(n_t):
        lp[j, 0] = part[j * piece : (j + 1) * piece]
        lp[j, 1] = jnp.broadcast_to(sq[j * piece : (j + 1) * piece], (piece, experts))

    def lp_send(i, carry):
        p = t_peer(i)
        rcopy(lp.at[p], lr.at[t], lp_s, lp_r, (d, p, s)).start()
        return carry

    lax.fori_loop(1, n_t, lp_send, 0)
    later(wait_bytes, lr.at[pl.ds(0, n_t - 1)], lp_s)
    lr[t] = lp[t]
    wait_bytes(wt, wt_r)
    own_down.wait()

    right, left = t_peer(1), t_peer(n_t - 1)
    hops = gather_hops

    def ring(g, hop, direction, h, incoming):
        step = hop if incoming else hop - 1
        origin = t_peer((n_t - step) % n_t) if direction == 0 else t_peer(step)
        ref = ag[g].at[origin, h]
        k = (direction * hops + hop - 1) * 2 + h
        return origin, rcopy(
            ref, ref, ag_s.at[g, k], ag_r.at[g, k], (d, right if direction == 0 else left, s)
        )

    def ring_start(g, hop, direction, h):
        c = ring(g, hop, direction, h, False)[1]
        c.start()
        later(c.wait_send)

    def legs(hop):
        if hop < hops:
            return [(h, direction) for h in range(2) for direction in range(2)]
        return [(0, 0), (1, 1)]

    def unpack(src, ns, use):
        pr = plane_rows(ns, chunks)
        tmp[: n_dp * pr] = src[...].astype(F32).reshape(n_dp * pr, LANE)
        for q in range(ns):
            use(q, [tmp[pl.ds(c * ns + q, n_dp, stride=pr), :] for c in range(chunks)])

    def group_of(q):
        for g, (s0, ns) in enumerate(groups):
            if s0 <= q < s0 + ns:
                return g, slice((q - s0) * n_dp, (q - s0 + 1) * n_dp)

    def do_rows():
        exchange_wait(recv[0], dis_r.at[0])
        squares = []

        def scale(q, cols):
            squares.append(sum(v * v for v in cols))
            g, at = group_of(q)
            for c, v in enumerate(cols):
                h, l0 = c // per_half, (c % per_half) * LANE
                ag[g][t, h, at, l0 : l0 + LANE] = (v * gn[h][0:1, l0 : l0 + LANE]).astype(BF)

        unpack(recv[0], slots, scale)
        for g in range(ng):
            for h, direction in legs(1):
                ring_start(g, 1, direction, h)
        ones = jnp.ones((8, LANE), F32)
        for q in range(slots):
            ss[t, :, q * n_dp : (q + 1) * n_dp] = dot(ones, squares[q], NT, precision=HIGH)

        def ss_send(i, carry):
            rcopy(ss.at[t], ss.at[t], ss_s, ss_r, (d, t_peer(i), s)).start()
            return carry

        lax.fori_loop(1, n_t, ss_send, 0)
        later(wait_bytes, ss.at[pl.ds(0, n_t - 1)], ss_s)
        for g in range(ng):
            acc[g][...] = dot(wt[t, 0], ag[g][t, 0], NT) + dot(wt[t, 1], ag[g][t, 1], NT)

    def do_farsend(j):
        swaps[j].wait_recv()
        dispatch(1 + j, [far[j, h] for h in range(2)])

    def do_far(j):
        exchange_wait(recv[1 + j], dis_r.at[1 + j])
        origins = [t_peer(half_way)] * 2 if j == 0 else [t_peer(gather_hops), t_peer(n_t - gather_hops)]

        def keep(q, cols):
            g, at = group_of(q)
            for c, v in enumerate(cols):
                h, l0 = c // per_half, (c % per_half) * LANE
                ag[g][origins[h], h, at, l0 : l0 + LANE] = v.astype(BF)

        unpack(recv[1 + j], slots, keep)
        for g in range(ng):
            for h, o in enumerate(origins):
                acc[g][...] += dot(wt[o, h], ag[g][o, h], NT)

    def do_gather(g, hop):
        going = legs(hop + 1) if hop < hops else []
        for h, direction in legs(hop):
            origin, c = ring(g, hop, direction, h, True)
            c.wait_recv()
            if (h, direction) in going:
                ring_start(g, hop + 1, direction, h)
            acc[g][...] += dot(wt[origin, h], ag[g][origin, h], NT)

    half = hid_n // 2

    def unit_legs(hop):
        if hop < unit_hops:
            return [(h, direction) for h in range(2) for direction in range(2)]
        return [(0, 0), (1, 1)]

    def units(g, hop, direction, h, incoming):
        step = hop if incoming else hop - 1
        origin = t_peer((n_t - step) % n_t) if direction == 0 else t_peer(step)
        ref = hid[g].at[origin, pl.ds(h * half, half)]
        k = (direction * unit_hops + hop - 1) * 2 + h
        return origin, rcopy(
            ref, ref, hid_s.at[g, k], hid_r.at[g, k], (d, right if direction == 0 else left, s)
        )

    def units_start(g, hop, direction, h):
        c = units(g, hop, direction, h, False)[1]
        c.start()
        later(c.wait_send)

    def do_hidden(g):
        s0, ns = groups[g]
        cols = slice(s0 * n_dp, (s0 + ns) * n_dp)
        if g == 0:
            wait_bytes(ss.at[pl.ds(0, n_t - 1)], ss_r)
        total = ss[0, 0:1, cols]
        for j in range(1, n_t):
            total = total + ss[j, 0:1, cols]
        rinv = lax.rsqrt(total / width + 1e-06)
        gate = acc[g][0:hid_n] * rinv
        hid[g][t] = (gate * jax.nn.sigmoid(gate) * (acc[g][hid_n : 2 * hid_n] * rinv)).astype(BF)
        for h, direction in unit_legs(1):
            units_start(g, 1, direction, h)
        if g == 0:
            wait_bytes(wdb.at[pl.ds(0, n_t - 1)], wd_r)
        oacc[g][...] = dot(hid[g][t], wdb[t], TN)

    def do_units(g, hop):
        got = [None, None]
        going = unit_legs(hop + 1) if hop < unit_hops else []
        for h, direction in unit_legs(hop):
            origin, c = units(g, hop, direction, h, True)
            c.wait_recv()
            got[direction] = origin
            if (h, direction) in going:
                units_start(g, hop + 1, direction, h)
        for origin in got if hop < unit_hops else got[:1]:
            oacc[g][...] += dot(hid[g][origin], wdb[origin], TN)

    def do_back(g):
        pack(lambda c: oacc[g][:, c * LANE : (c + 1) * LANE], groups[g][1], send2[g])
        exchange(send2[g], recv2[g], ret_s.at[g], ret_r.at[g])

    def do_logits():
        wait_bytes(lr.at[pl.ds(0, n_t - 1)], lp_r)
        tot = lr[0]
        for j in range(1, n_t):
            tot = tot + lr[j]
        lg[t] = tot[0] * lax.rsqrt(tot[1] / width + 1e-06)

        def lg_send(i, carry):
            rcopy(lg.at[t], lg.at[t], lg_s, lg_r, (d, t_peer(i), s)).start()
            return carry

        lax.fori_loop(1, n_t, lg_send, 0)
        later(wait_bytes, lg.at[pl.ds(0, n_t - 1)], lg_s)

    def do_weights():
        r_of = lax.broadcasted_iota(jnp.int32, (experts, rows), 1)
        expand_t = jnp.where(
            lax.broadcasted_iota(jnp.int32, (experts, rows), 0) == 2 * (r_of % n_dp) + s, 1.0, 0.0
        ).astype(BF)
        slot_of = lax.broadcasted_iota(jnp.int32, (toks, rows), 1) // n_dp + 1
        mine = dot(taken, expand_t, TN) == slot_of.astype(F32)
        wait_bytes(lg.at[pl.ds(0, n_t - 1)], lg_r)
        logits = jnp.concatenate([lg[j] for j in range(n_t)], axis=0).T
        masked = jnp.where(onehot > 0.0, logits, -jnp.inf)
        ex = jnp.exp(masked - jnp.max(masked, axis=0, keepdims=True))
        weights = ex / jnp.sum(ex, axis=0, keepdims=True)
        w_hi = weights.astype(BF)
        w_lo = (weights - w_hi.astype(F32)).astype(BF)
        ct[0] = jnp.where(mine, dot(w_hi, expand_t, TN), 0.0).astype(BF)
        ct[1] = jnp.where(mine, dot(w_lo, expand_t, TN), 0.0).astype(BF)

    does = {"logits": do_logits, "weights": do_weights, "rows": do_rows, "far": do_far, "farsend": do_farsend, "gather": do_gather, "hidden": do_hidden, "units": do_units, "back": do_back}
    for name, *args in schedule(ng, gather_hops, unit_hops):
        does[name](*args)

    for g, (s0, ns) in enumerate(groups):
        exchange_wait(recv2[g], ret_r.at[g])

        def keep(q, cols):
            for c, v in enumerate(cols):
                oacc[g][q * n_dp : (q + 1) * n_dp, c * LANE : (c + 1) * LANE] = v

        unpack(recv2[g], ns, keep)
        for h in range(2):
            z = oacc[g][:, h * feats : (h + 1) * feats].astype(BF)
            cols = slice(s0 * n_dp, (s0 + ns) * n_dp)
            m = dot(ct[0, :, cols], z) + dot(ct[1, :, cols], z)
            mixs[h] = m if g == 0 else mixs[h] + m
    last = rcopy(mixs.at[other], mixr, mix_s, mix_r, (d, t, other))
    last.start()
    last.wait_recv()
    out[...] = (mixs[s] + mixr[...]).astype(BF)
    later(last.wait_send)

    for f in left_over:
        f()


def body(tokens, gain, router, routes, w_gate, w_up, w_down):
    toks, feats = tokens.shape
    top = routes.shape[1]
    n_dp, n_t, n_side = (lax.axis_size(a) for a in ("dp", "tensor", "side"))
    experts = n_dp * n_side
    slots = min(toks, max(2, toks * top * 5 // (experts * 4)))
    hid_n = w_gate.shape[2]
    groups = split_slots(slots)
    chunks = 2 * feats // LANE
    n_rows = [ns * n_dp for _, ns in groups]
    planes = [plane_rows(ns, chunks) for _, ns in groups]
    plane = plane_rows(slots, chunks)
    rows = slots * n_dp
    gather_hops, unit_hops = n_t // 2 - 1, n_t // 2
    piece = toks // n_t
    cfg = (n_dp, n_t, slots, groups, toks, feats, experts, top, hid_n)
    vm = pltpu.VMEM
    dma = pltpu.SemaphoreType.DMA
    ng = len(groups)
    plane_bufs = [vm((n_dp, p, LANE), BF) for p in planes]
    scratch = (
        [
            vm((2, toks, feats), BF),
            vm((toks, feats), BF),
            vm((2, 2, toks, feats), BF),
            vm((toks, feats), BF),
            vm((hid_n, 2 * feats), BF),
            vm((2, feats, experts), BF),
            vm((2, 8, feats), F32),
            vm((rows, toks), BF),
            vm((n_dp * plane, LANE), F32),
            vm((n_t, 2, piece, experts), F32),
            vm((n_t, 2, piece, experts), F32),
            vm((n_t, piece, experts), F32),
            vm((n_t, 8, rows), F32),
            vm((n_t, 2, 2 * hid_n, feats), BF),
            vm((n_t, hid_n, 2 * feats), BF),
            vm((2, toks, rows), BF),
            vm((2, toks, feats), F32),
            vm((toks, feats), F32),
        ]
        + [vm((n_dp, plane, LANE), BF)] * 6
        + plane_bufs * 2
        + [vm((n_t, hid_n, n), BF) for n in n_rows]
        + [vm((n, 2 * feats), F32) for n in n_rows]
        + [vm((n_t, 2, n, feats), BF) for n in n_rows]
        + [vm((2 * hid_n, n), F32) for n in n_rows]
        + [dma((3,)), dma((3,)), dma((7,)), dma((7,))]
        + [dma] * 10
        + [dma((3,))] * 2
        + [dma((ng,))] * 2
        + [dma] * 2
        + [dma((ng, 4 * gather_hops))] * 2
        + [dma((ng, 4 * unit_hops))] * 2
    )
    in_vmem, in_hbm = pl.BlockSpec(memory_space=vm), pl.BlockSpec(memory_space=pl.ANY)
    return pl.pallas_call(
        functools.partial(kernel, cfg),
        out_shape=jax.ShapeDtypeStruct((toks, feats), BF),
        in_specs=[in_vmem] * 4 + [in_hbm] * 3,
        out_specs=in_vmem,
        scratch_shapes=scratch,
        compiler_params=pltpu.CompilerParams(
            collective_id=0, has_side_effects=True, vmem_limit_bytes=56 * 1024 * 1024
        ),
        name="routed_experts",
    )(
        tokens,
        gain,
        router,
        routes.T,
        jnp.swapaxes(w_gate, 1, 2),
        jnp.swapaxes(w_up, 1, 2),
        w_down,
    )


def solution(mesh):
    placed = (
        P("dp", ("tensor", "side")),
        P(("tensor", "side")),
        P(("tensor", "side"), None),
        P("dp", None),
        P(("dp", "side"), None, "tensor"),
        P(("dp", "side"), None, "tensor"),
        P(("dp", "side"), "tensor", None),
    )
    return jax.shard_map(
        body, mesh=mesh, in_specs=placed, out_specs=P("dp", ("tensor", "side")), check_vma=False
    )
```
